256 devices in a mesh: rep: 16 (over z_hi, x), fsdp: 16 (over z_lo, y, core).
Axes of the slice: x: 4, y: 4, z: 8 (z_hi: 4, z_lo: 2; z = z_hi * 2 + z_lo), core: 2. Of those that a mesh axis runs over, the one named last changes fastest.
Arguments:
- anchor: float32 [16, 128, 25600], P('rep', 'fsdp'), may hold values from -6 to 6
- momentum: float32 [16, 128, 25600], P('rep', 'fsdp'), may hold values from -4 to 4
- adam_first: float32 [16, 128, 25600], P('rep', 'fsdp'), may hold values from -4 to 4
- adam_second: float32 [16, 128, 25600], P('rep', 'fsdp'), may hold values from 0.05 to 2
- gradients: bfloat16 [2, 16, 128, 25600], P(None, 'rep', 'fsdp'), may hold values from -6 to 6
- probe_tokens: bfloat16 [2, 16, 1024, 128], P(None, 'rep', 'fsdp'), may hold values from -0.52734375 to 0.52734375
- matching: int32 [2, 16], replicated, may hold values from 0 to 15, as said below
Outputs:
- anchor_out: float32 [16, 128, 25600], P('rep', 'fsdp')
- momentum_out: float32 [16, 128, 25600], P('rep', 'fsdp')
- evaluated: bfloat16 [2, 16, 1024, 25600], P(None, 'rep', 'fsdp')
The draws below stay inside these ranges and needn't reach their ends.
Inputs may be any that keep to these rules, and one draw needn't show every extreme that they name: In each outer step the matching pairs the replicas: matching[s, matching[s, r]] = r and matching[s, r] != r.
All inputs are finite; a program needn't handle non-finite values.
Results may differ from the reference program's by a relative error of at most 0.0049.
Values may be sent and summed in bfloat16 or wider, within the bound.
No kernel may reach another device: no remote copies, remote signals or barrier semaphores. Data moves between devices by JAX's collectives and lax.ppermute only.
A program may use at most 128 MiB of HBM per device.

```python
import math
import jax
import jax.numpy as jnp
from jax import lax

FF = 25600
STEPS = 2
INNER = 4
REP = 16
D_ROWS = 128
TOKENS = 1024


def draw_matching(key, part):
    key = jax.random.fold_in(key, 7)
    matchings = []
    for outer_step in range(STEPS):
        shuffled = jax.random.permutation(jax.random.fold_in(key, outer_step), REP).astype(jnp.int32)
        firsts = shuffled[0::2]
        seconds = shuffled[1::2]
        partner = jnp.zeros((REP,), jnp.int32).at[firsts].set(seconds).at[seconds].set(firsts)
        matchings.append(partner)
    return jnp.stack(matchings).astype(jnp.int32)


def block_levels(own_key, dims, split, low, largest):
    def one(axis_at, shards_of):
        draws = jax.random.uniform(jax.random.fold_in(jax.random.fold_in(own_key, 6), axis_at), (shards_of,), jnp.float32, low / len(split), largest / len(split))
        return jnp.repeat(jnp.exp(draws), dims[axis_at] // shards_of).reshape((-1,) + (1,) * (len(dims) - axis_at - 1))

    level = one(*split[0])
    for cut in split[1:]:
        level = level * one(*cut)
    return level


def normal_values(own_key, shape, spread, bound, cuts=(), dtype=jnp.bfloat16):
    drawn = spread * jax.random.normal(own_key, shape, jnp.float32)
    if cuts:
        drawn = drawn * block_levels(own_key, shape, cuts, -0.22, 0.18)
    return jnp.clip(drawn, -bound, bound).astype(dtype)


def setup_inputs(seed: int = 0) -> dict:
    key_of = jax.random.split(jax.random.key(seed), 8)
    return {
        "anchor": normal_values(key_of[0], (REP, D_ROWS, FF), 1.0, 6.0, ((0, 16), (1, 16)), jnp.float32),
        "momentum": normal_values(key_of[1], (REP, D_ROWS, FF), 0.3, 4.0, ((0, 16), (1, 16)), jnp.float32),
        "adam_first": normal_values(key_of[2], (REP, D_ROWS, FF), 0.3, 4.0, ((0, 16), (1, 16)), jnp.float32),
        "adam_second": jnp.clip(jnp.exp(math.log(2.0) - 3.6888794 * jax.random.uniform(key_of[3], (REP, D_ROWS, FF), jnp.float32) ** block_levels(key_of[3], (REP, D_ROWS, FF), ((0, 16), (1, 16)), -0.2, 0.2)), 0.05, 2.0),
        "gradients": normal_values(key_of[4], (STEPS, REP, D_ROWS, FF), 1.0, 6.0, ((1, 16), (2, 16))),
        "probe_tokens": normal_values(key_of[5], (STEPS, REP, TOKENS, D_ROWS), (D_ROWS ** -0.5), 0.52734375, ((1, 16), (2, 16))),
        "matching": draw_matching(jax.random.fold_in(key_of[7], 71), 0),
    }


first_decay = 0.9
second_decay = 0.95
inner_rate = 0.2
weight_decay = 0.1
outer_rate = 0.7
outer_beta = 0.9
epsilon = 1e-08

def evaluate_one(operands):
    return jnp.dot(operands[0], operands[1], preferred_element_type=jnp.float32).astype(jnp.bfloat16)

def reference(anchor, momentum, adam_first, adam_second, gradients, probe_tokens, matching):
    first_moment = adam_first
    second_moment = adam_second
    evaluations = []
    for outer_step in range(STEPS):
        partners = matching[outer_step].astype(jnp.int32)
        mixed = 0.5 * (anchor + jnp.take(anchor, partners, axis=0))
        carried = 0.5 * (momentum + jnp.take(momentum, partners, axis=0))
        gradient = gradients[outer_step].astype(jnp.float32)
        inner_weights = mixed
        for inner_pass in range(INNER):
            first_moment = first_decay * first_moment + (1.0 - first_decay) * gradient
            second_moment = second_decay * second_moment + (1.0 - second_decay) * gradient * gradient
            inner_weights = inner_weights - inner_rate * (first_moment / (jnp.sqrt(second_moment) + epsilon) + weight_decay * inner_weights)
        momentum = outer_beta * carried + (mixed - inner_weights)
        anchor = mixed - outer_rate * momentum
        weights = anchor.astype(jnp.bfloat16)
        evaluations.append(lax.map(evaluate_one, (probe_tokens[outer_step], weights)))
    return (anchor, momentum, jnp.stack(evaluations))
```

```python
import functools

import jax
import jax.numpy as jnp
from jax import lax
from jax.experimental import pallas as pl
from jax.experimental.pallas import tpu as pltpu
from jax.sharding import PartitionSpec as P

INNER = 4
first_decay = 0.9
second_decay = 0.95
inner_rate = 0.2
weight_decay = 0.1
outer_rate = 0.7
outer_beta = 0.9
epsilon = 1e-08

SHRINK = 1.0 - inner_rate * weight_decay
KEEP = SHRINK**INNER
Z_OF_W = 1.0 - outer_rate * (1.0 - KEEP)
Z_OF_U = -outer_rate * outer_beta
Y_OF_W = 1.0 - KEEP
Y_OF_U = outer_beta

LANES = 128
SLABS = 8
F32 = jnp.float32
BF16 = jnp.bfloat16
VMEM_LIMIT = 14 * 1024 * 1024
PACK_LIMIT = 58 * 1024 * 1024


def params(limit=VMEM_LIMIT):
    return pltpu.CompilerParams(vmem_limit_bytes=limit)


def cost(flops, moved):
    return pl.CostEstimate(flops=int(flops), bytes_accessed=int(moved), transcendentals=0)


def adam(first, second, gradient):
    moved = (1.0 - first_decay) * gradient
    squared = (1.0 - second_decay) * gradient * gradient
    total = None
    for inner_pass in range(INNER):
        first = first_decay * first + moved
        second = second_decay * second + squared
        step = first / (jnp.sqrt(second) + epsilon)
        total = step if total is None else SHRINK * total + step
    return first, second, inner_rate * total


def windows(columns, window):
    slab = columns // SLABS
    return [start for j in range(SLABS) for start in (j * slab, (j + 1) * slab - window)]


def pack_kernel(*refs):
    sources, (packed_ref, d_out), held, arrived = refs[:5], refs[5:7], refs[7:12], refs[12]
    columns, window = d_out.shape[1], packed_ref.shape[3]
    slab = columns // SLABS
    starts = windows(columns, window)
    copies = []
    for j in range(SLABS):
        lanes = pl.ds(j * slab, slab)
        for i, (source, kept) in enumerate(zip(sources, held)):
            piece = source.at[0, 0, :, lanes] if i == 4 else source.at[0, :, lanes]
            copies.append(pltpu.make_async_copy(piece, kept.at[j], arrived.at[j, i]))
            copies[-1].start()
    for j in range(SLABS):
        lanes = pl.ds(j * slab, slab)
        for copy in copies[5 * j : 5 * j + 5]:
            copy.wait()
        w, u, m, v, g = (kept[j] for kept in held)
        d = adam(m, v, g.astype(F32))[2]
        d_out[:, lanes] = d
        sent = (Z_OF_W * w + Z_OF_U * u, Y_OF_U * u + Y_OF_W * w, d)
        for relay in (2 * j, 2 * j + 1):
            start = starts[relay] - j * slab
            for which, value in enumerate(sent):
                packed_ref[relay, which] = value[:, start : start + window].astype(BF16)


def second_kernel(m_ref, v_ref, g_ref, d_out):
    columns = d_out.shape[1]
    slab = columns // SLABS
    for j in range(SLABS):
        lanes = pl.ds(j * slab, slab)
        first, second = m_ref[0, :, lanes], v_ref[0, :, lanes]
        gradient = g_ref[0, 0, :, lanes].astype(F32)
        for _ in range(INNER):
            first = first_decay * first + (1.0 - first_decay) * gradient
            second = second_decay * second + (1.0 - second_decay) * gradient * gradient
        d_out[:, lanes] = adam(first, second, g_ref[1, 0, :, lanes].astype(F32))[2]


def mean(got_ref, which, r, p):
    return 0.5 * (got_ref[r, which].astype(F32) + got_ref[p, which].astype(F32))


def after_first_step(got_ref, r, p, of_w, of_u):
    shared = mean(got_ref, 0, r, p)
    d = got_ref[r, 2].astype(F32)
    return of_w * (shared - outer_rate * d) + of_u * (mean(got_ref, 1, r, p) + d), shared


def relay_kernel(matching_ref, got_ref, d_ref, tokens_ref, back_ref, held_ref):
    replicas = got_ref.shape[0]

    @pl.loop(0, replicas)
    def _(r):
        held_ref[r], shared = after_first_step(got_ref, r, matching_ref[0, r], Z_OF_W, Z_OF_U)
        back_ref[r, 0] = shared.astype(BF16)

    @pl.loop(0, replicas)
    def _(r):
        back_ref[r, 1] = (0.5 * (held_ref[r] + held_ref[matching_ref[1, r]])).astype(BF16)


def momentum_relay_kernel(matching_ref, got_ref, after_ref, back_ref, held_ref):
    replicas = got_ref.shape[0]

    @pl.loop(0, replicas)
    def _(r):
        held_ref[r] = after_first_step(got_ref, r, matching_ref[0, r], Y_OF_W, Y_OF_U)[0]

    @pl.loop(0, replicas)
    def _(r):
        back_ref[r] = (0.5 * (held_ref[r] + held_ref[matching_ref[1, r]])).astype(BF16)


def joined(first, last, slab):
    overlap = first.shape[1] + last.shape[1] - slab
    return jnp.concatenate([first, last[:, overlap:]], axis=1).astype(F32)


def weights_kernel(core_ref, back_ref, d1_ref, d2_ref, *refs):
    parts, w_ref = refs[:4], refs[4]
    slab = d1_ref.shape[1] // SLABS
    for j in range(SLABS):
        lanes = pl.ds(j * slab, slab)
        first, second = (joined(back_ref[2 * j, i], back_ref[2 * j + 1, i], slab) for i in range(2))
        first = first - outer_rate * d1_ref[:, lanes]
        second = second - outer_rate * d2_ref[:, lanes]
        w_ref[0, :, lanes] = second
        quarter, lanes = j % (SLABS // 2) // 2, pl.ds(j % 2 * slab, slab)
        mine = core_ref[0] == j // (SLABS // 2)
        for away, chosen in enumerate((mine, jnp.logical_not(mine))):
            part = parts[2 * quarter + away]

            @pl.when(chosen)
            def _(part=part, lanes=lanes, first=first, second=second):
                part[0, :, lanes] = first.astype(BF16)
                part[1, :, lanes] = second.astype(BF16)


def momentum_kernel(back_ref, d_ref, u_ref):
    slab = d_ref.shape[1] // SLABS
    for j in range(SLABS):
        lanes = pl.ds(j * slab, slab)
        u_ref[0, :, lanes] = joined(back_ref[2 * j], back_ref[2 * j + 1], slab) + d_ref[:, lanes]


def copy_kernel(from_ref, after_ref, to_ref):
    for step in range(to_ref.shape[0]):
        to_ref[step] = from_ref[step]


def chip_kernel(*refs):
    pieces, out = refs[:4], refs[-1]
    for i, piece in enumerate(pieces):
        for step in range(out.shape[0]):
            out[step, i] = piece[step]


TILES = 5


def evaluate_kernel(quarter, core_ref, tokens_ref, *refs):
    blocks, (out_ref, sent_ref, own_ref, done) = refs[:4], refs[-4:]
    steps, tokens, width = sent_ref.shape
    tile = width // TILES
    start = pl.multiple_of(core_ref[0] * (2 * width) + quarter * width, LANES)
    copies = []
    for step in range(steps):
        for j in range(TILES):
            lanes = pl.ds(j * tile, tile)
            rows = jnp.concatenate([block[step, i, :, lanes] for block in blocks for i in range(4)], axis=0)
            product = jnp.dot(tokens_ref[step], rows, preferred_element_type=F32).astype(BF16)
            own_ref[step, :, lanes] = product[:tokens]
            sent_ref[step, :, lanes] = product[tokens:]
            copies.append(
                pltpu.make_async_copy(
                    own_ref.at[step, :, lanes],
                    out_ref.at[step, 0, :, pl.ds(pl.multiple_of(start + j * tile, LANES), tile)],
                    done.at[step, j],
                )
            )
            copies[-1].start()
    for copy in copies:
        copy.wait()


def place_kernel(quarter, core_ref, piece_ref, buffer_ref, out_ref, done):
    steps, _, width = piece_ref.shape
    tile = width // TILES
    start = pl.multiple_of((1 - core_ref[0]) * (2 * width) + quarter * width, LANES)
    copies = []
    for step in range(steps):
        for j in range(TILES):
            copies.append(
                pltpu.make_async_copy(
                    piece_ref.at[step, :, pl.ds(j * tile, tile)],
                    out_ref.at[step, 0, :, pl.ds(pl.multiple_of(start + j * tile, LANES), tile)],
                    done.at[step, j],
                )
            )
            copies[-1].start()
    for copy in copies:
        copy.wait()


def shards(anchor, momentum, adam_first, adam_second, gradients, probe_tokens, matching):
    replicas = lax.axis_size("rep")
    group = lax.axis_size("fsdp")
    _, rows, columns = anchor.shape
    steps, _, tokens, depth = probe_tokens.shape
    slab = columns // SLABS
    window = LANES * (-(-slab // (2 * LANES)))
    quarter = columns // 4
    unit = rows * columns
    ring = group // 4
    place = lax.axis_index("fsdp")
    core = lax.rem(place, 2).astype(jnp.int32)
    core_ref = core[None]

    whole = pl.BlockSpec(memory_space=pltpu.VMEM)
    scalar = pl.BlockSpec(memory_space=pltpu.SMEM)
    far = pl.BlockSpec(memory_space=pltpu.HBM)
    loose = pl.BlockSpec(memory_space=pl.ANY)
    flat = jax.ShapeDtypeStruct((rows, columns), F32)
    whole_out = jax.ShapeDtypeStruct((1, rows, columns), F32)
    part = jax.ShapeDtypeStruct((steps, rows, quarter), BF16)
    chip = jax.ShapeDtypeStruct((steps, 4, rows, quarter), BF16)
    moved = jax.ShapeDtypeStruct((replicas, 3, rows, window), BF16)
    two_backs = jax.ShapeDtypeStruct((replicas, 2, rows, window), BF16)
    one_back = jax.ShapeDtypeStruct((replicas, rows, window), BF16)
    products = jax.ShapeDtypeStruct((steps, 1, tokens, columns), BF16)
    sent_products = jax.ShapeDtypeStruct((steps, tokens, quarter), BF16)

    def call(kernel, name, in_specs, out_specs, out_shape, flops, nbytes, limit=VMEM_LIMIT, **rest):
        return pl.pallas_call(
            kernel,
            in_specs=in_specs,
            out_specs=out_specs,
            out_shape=out_shape,
            compiler_params=params(limit),
            cost_estimate=cost(flops, nbytes),
            name=name,
            **rest,
        )

    def at(z, y, c):
        return (z * ring + y % ring) * 2 + c

    def permute(value, dz=0, dy=0, dc=0):
        pairs = [
            (at(z, y, c), at(z ^ dz, y + dy, c ^ dc))
            for z in range(2)
            for y in range(ring)
            for c in range(2)
        ]
        return lax.ppermute(value, "fsdp", pairs)

    def relayed(value):
        return lax.all_to_all(value, "rep", 0, 0, tiled=True)

    z_at, y_at = place // (2 * ring), (place // 2) % ring
    owners = jnp.stack(
        [
            ((z_at ^ dz) * ring + (y_at + dy) % ring) * 2 + (core ^ dc)
            for dy in (0, -1, 1, 2)
            for dz in range(2)
            for dc in range(2)
        ]
    )
    own_tokens = probe_tokens[:, 0]
    chip_tokens = jnp.concatenate([own_tokens, permute(own_tokens, dc=1)], axis=1)
    chip_tokens = jnp.take(
        chip_tokens.reshape(steps, 2 * tokens, group, depth // group), owners, axis=2
    ).reshape(steps, 2 * tokens, depth)

    packed, d1 = call(
        pack_kernel,
        "pack",
        [far] * 5,
        [whole] * 2,
        [moved, flat],
        100 * unit,
        26 * unit,
        PACK_LIMIT,
        scratch_shapes=[pltpu.VMEM((SLABS, rows, slab), t) for t in (F32, F32, F32, F32, BF16)]
        + [pltpu.SemaphoreType.DMA((SLABS, 5))],
    )(anchor, momentum, adam_first, adam_second, gradients)
    got = relayed(packed)
    d2 = call(second_kernel, "second", [whole] * 3, whole, flat, 120 * unit, 14 * unit)(
        adam_first, adam_second, gradients
    )

    back = call(
        relay_kernel,
        "relay",
        [scalar, whole, loose, loose],
        whole,
        two_backs,
        30 * unit,
        10 * unit,
        scratch_shapes=[pltpu.VMEM((replicas, rows, window), F32)],
    )(matching, got, d2, chip_tokens)
    kept_low, sent_low, kept_high, sent_high, anchor_out = call(
        weights_kernel,
        "weights",
        [scalar, whole, whole, whole],
        [whole] * 5,
        [part] * 4 + [whole_out],
        8 * unit,
        24 * unit,
    )(core_ref, relayed(back), d1, d2)

    def chip_rows(kept, sent, *after):
        pieces = kept, permute(sent, dc=1), permute(kept, dz=1), permute(sent, dz=1, dc=1)
        return call(
            chip_kernel, "chip", [whole] * 4 + [loose] * len(after), whole, chip, 0, 8 * unit
        )(*pieces, *after)

    low = chip_rows(kept_low, sent_low)
    low_up, low_down = permute(low, dy=1), permute(low, dy=-1)
    low_far = permute(low_up, dy=1)
    high = chip_rows(kept_high, sent_high, low_up, low_down)
    high_down = permute(high, dy=-1)
    later_high = call(copy_kernel, "later", [whole, loose], whole, chip, 0, 8 * unit)(high, low_far)
    high_up = permute(later_high, dy=1)
    high_far = permute(high_down, dy=-1)
    last = call(
        momentum_relay_kernel,
        "momentum_relay",
        [scalar, whole, loose],
        whole,
        one_back,
        30 * unit,
        8 * unit,
        scratch_shapes=[pltpu.VMEM((replicas, rows, window), F32)],
    )(matching, got, later_high)
    momentum_out = call(momentum_kernel, "momentum", [whole] * 2, whole, whole_out, 2 * unit, 10 * unit)(
        relayed(last), d2
    )

    def evaluate(at_quarter, blocks, buffer, *after):
        kernel = functools.partial(evaluate_kernel, at_quarter)
        operands = [core_ref, chip_tokens, *blocks, *after]
        in_specs = [scalar] + [whole] * 5 + [loose] * len(after)
        aliases = {}
        if buffer is not None:
            aliases = {len(operands): 0}
            operands.append(buffer)
            in_specs.append(far)
        return call(
            kernel,
            "evaluate",
            in_specs,
            [far, whole],
            [products, sent_products],
            8 * tokens * depth * quarter,
            16 * unit,
            input_output_aliases=aliases,
            scratch_shapes=[
                pltpu.VMEM((steps, tokens, quarter), BF16),
                pltpu.SemaphoreType.DMA((steps, TILES)),
            ],
        )(*operands)

    def put(at_quarter, piece, buffer):
        return call(
            functools.partial(place_kernel, at_quarter),
            "place",
            [scalar, whole, far],
            far,
            products,
            0,
            8 * unit,
            input_output_aliases={2: 0},
            scratch_shapes=[pltpu.SemaphoreType.DMA((steps, TILES))],
        )(core_ref, piece, buffer)

    buffer, low_sent = evaluate(0, (low, low_up, low_down, low_far), None, later_high)
    buffer, high_sent = evaluate(1, (high, high_up, high_down, high_far), buffer, momentum_out)
    buffer = put(0, permute(low_sent, dc=1), buffer)
    buffer = put(1, permute(high_sent, dc=1), buffer)
    return anchor_out, momentum_out, buffer


def solution(mesh):
    placed = (
        P("rep", "fsdp", None),
        P("rep", "fsdp", None),
        P("rep", "fsdp", None),
        P("rep", "fsdp", None),
        P(None, "rep", "fsdp", None),
        P(None, "rep", "fsdp", None),
        P(),
    )
    return jax.shard_map(
        shards,
        mesh=mesh,
        in_specs=placed,
        out_specs=(P("rep", "fsdp", None), P("rep", "fsdp", None), P(None, "rep", "fsdp", None)),
        check_vma=False,
    )
```

```python
import functools

import jax
import jax.numpy as jnp
from jax import lax
from jax.experimental import pallas as pl
from jax.experimental.pallas import tpu as pltpu
from jax.sharding import PartitionSpec as P

INNER = 4
first_decay = 0.9
second_decay = 0.95
inner_rate = 0.2
weight_decay = 0.1
outer_rate = 0.7
outer_beta = 0.9
epsilon = 1e-08

SHRINK = 1.0 - inner_rate * weight_decay
KEEP = SHRINK**INNER
Z_OF_W = 1.0 - outer_rate * (1.0 - KEEP)
Z_OF_U = -outer_rate * outer_beta
Y_OF_W = 1.0 - KEEP
Y_OF_U = outer_beta

LANES = 128
SLABS = 8
F32 = jnp.float32
BF16 = jnp.bfloat16
VMEM_LIMIT = 14 * 1024 * 1024
PACK_LIMIT = 58 * 1024 * 1024


def params(limit=VMEM_LIMIT):
    return pltpu.CompilerParams(vmem_limit_bytes=limit)


def cost(flops, moved):
    return pl.CostEstimate(flops=int(flops), bytes_accessed=int(moved), transcendentals=0)


def adam(first, second, gradient):
    moved = (1.0 - first_decay) * gradient
    squared = (1.0 - second_decay) * gradient * gradient
    total = None
    for inner_pass in range(INNER):
        first = first_decay * first + moved
        second = second_decay * second + squared
        step = first / (jnp.sqrt(second) + epsilon)
        total = step if total is None else SHRINK * total + step
    return first, second, inner_rate * total


def windows(columns, window):
    slab = columns // SLABS
    return [start for j in range(SLABS) for start in (j * slab, (j + 1) * slab - window)]


def pack_kernel(*refs):
    sources, (packed_ref, d_out), held, arrived = refs[:5], refs[5:7], refs[7:12], refs[12]
    columns, window = d_out.shape[1], packed_ref.shape[3]
    slab = columns // SLABS
    starts = windows(columns, window)
    copies = []
    for j in range(SLABS):
        lanes = pl.ds(j * slab, slab)
        for i, (source, kept) in enumerate(zip(sources, held)):
            piece = source.at[0, 0, :, lanes] if i == 4 else source.at[0, :, lanes]
            copies.append(pltpu.make_async_copy(piece, kept.at[j], arrived.at[j, i]))
            copies[-1].start()
    for j in range(SLABS):
        lanes = pl.ds(j * slab, slab)
        for copy in copies[5 * j : 5 * j + 5]:
            copy.wait()
        w, u, m, v, g = (kept[j] for kept in held)
        d = adam(m, v, g.astype(F32))[2]
        d_out[:, lanes] = d
        sent = (Z_OF_W * w + Z_OF_U * u, Y_OF_U * u + Y_OF_W * w, d)
        for relay in (2 * j, 2 * j + 1):
            start = starts[relay] - j * slab
            for which, value in enumerate(sent):
                packed_ref[relay, which] = value[:, start : start + window].astype(BF16)


def second_kernel(m_ref, v_ref, g_ref, d_out):
    columns = d_out.shape[1]
    slab = columns // SLABS
    for j in range(SLABS):
        lanes = pl.ds(j * slab, slab)
        first, second = m_ref[0, :, lanes], v_ref[0, :, lanes]
        gradient = g_ref[0, 0, :, lanes].astype(F32)
        for _ in range(INNER):
            first = first_decay * first + (1.0 - first_decay) * gradient
            second = second_decay * second + (1.0 - second_decay) * gradient * gradient
        d_out[:, lanes] = adam(first, second, g_ref[1, 0, :, lanes].astype(F32))[2]


def mean(got_ref, which, r, p):
    return 0.5 * (got_ref[r, which].astype(F32) + got_ref[p, which].astype(F32))


def after_first_step(got_ref, r, p, of_w, of_u):
    shared = mean(got_ref, 0, r, p)
    d = got_ref[r, 2].astype(F32)
    return of_w * (shared - outer_rate * d) + of_u * (mean(got_ref, 1, r, p) + d), shared


def relay_kernel(matching_ref, got_ref, d_ref, tokens_ref, back_ref, held_ref):
    replicas = got_ref.shape[0]

    @pl.loop(0, replicas)
    def _(r):
        held_ref[r], shared = after_first_step(got_ref, r, matching_ref[0, r], Z_OF_W, Z_OF_U)
        back_ref[r, 0] = shared.astype(BF16)

    @pl.loop(0, replicas)
    def _(r):
        back_ref[r, 1] = (0.5 * (held_ref[r] + held_ref[matching_ref[1, r]])).astype(BF16)


def momentum_relay_kernel(matching_ref, got_ref, *refs):
    back_ref, held_ref = refs[-2:]
    replicas = got_ref.shape[0]

    @pl.loop(0, replicas)
    def _(r):
        held_ref[r] = after_first_step(got_ref, r, matching_ref[0, r], Y_OF_W, Y_OF_U)[0]

    @pl.loop(0, replicas)
    def _(r):
        back_ref[r] = (0.5 * (held_ref[r] + held_ref[matching_ref[1, r]])).astype(BF16)


def joined(first, last, slab):
    overlap = first.shape[1] + last.shape[1] - slab
    return jnp.concatenate([first, last[:, overlap:]], axis=1).astype(F32)


def weights_kernel(core_ref, back_ref, d1_ref, d2_ref, *refs):
    parts, (own_ref, w_ref) = refs[:4], refs[4:]
    slab = d1_ref.shape[1] // SLABS
    for j in range(SLABS):
        lanes = pl.ds(j * slab, slab)
        first, second = (joined(back_ref[2 * j, i], back_ref[2 * j + 1, i], slab) for i in range(2))
        first = first - outer_rate * d1_ref[:, lanes]
        second = second - outer_rate * d2_ref[:, lanes]
        w_ref[0, :, lanes] = second
        quarter, lanes = j % (SLABS // 2) // 2, pl.ds(j % 2 * slab, slab)
        mine = core_ref[0] == j // (SLABS // 2)
        for away, chosen in enumerate((mine, jnp.logical_not(mine))):
            part = parts[2 * quarter + away]

            @pl.when(chosen)
            def _(part=part, lanes=lanes, first=first, second=second):
                part[0, :, lanes] = first.astype(BF16)
                part[1, :, lanes] = second.astype(BF16)

        @pl.when(mine)
        def _(quarter=quarter, lanes=lanes, first=first, second=second):
            own_ref[quarter, 0, :, lanes] = first.astype(BF16)
            own_ref[quarter, 1, :, lanes] = second.astype(BF16)


def momentum_kernel(back_ref, d_ref, u_ref):
    slab = d_ref.shape[1] // SLABS
    for j in range(SLABS):
        lanes = pl.ds(j * slab, slab)
        u_ref[0, :, lanes] = joined(back_ref[2 * j], back_ref[2 * j + 1], slab) + d_ref[:, lanes]


def onward_kernel(quarter, own_ref, others_ref, *refs):
    out_ref = refs[-1]
    for step in range(out_ref.shape[0]):
        out_ref[step, 0] = own_ref[quarter, step]
        for i in range(3):
            out_ref[step, i + 1] = others_ref[step, i]


def low_chip_kernel(*refs):
    chip_kernel(*refs[:3], refs[-3])
    for part, later in zip(refs[3:5], refs[-2:]):
        later[...] = part[...]


def chip_kernel(*refs):
    pieces, out = refs[:3], refs[-1]
    for i, piece in enumerate(pieces):
        for step in range(out.shape[0]):
            out[step, i] = piece[step]


TILES = 5


def evaluate_kernel(quarter, core_ref, tokens_ref, *refs):
    blocks, far_ref, (out_ref, sent_ref, own_ref, done) = refs[:6], refs[6], refs[-4:]
    steps, tokens, width = sent_ref.shape
    tile = width // TILES
    start = pl.multiple_of(core_ref[0] * (2 * width) + quarter * width, LANES)
    copies = []
    for step in range(steps):
        for j in range(TILES):
            lanes = pl.ds(j * tile, tile)
            rows = []
            for own, others in zip(blocks[::2], blocks[1::2]):
                rows.append(own[quarter, step, :, lanes])
                rows += [others[step, i, :, lanes] for i in range(3)]
            rows += [far_ref[step, i, :, lanes] for i in range(4)]
            rows = jnp.concatenate(rows, axis=0)
            product = jnp.dot(tokens_ref[step], rows, preferred_element_type=F32).astype(BF16)
            own_ref[step, :, lanes] = product[:tokens]
            sent_ref[step, :, lanes] = product[tokens:]
            copies.append(
                pltpu.make_async_copy(
                    own_ref.at[step, :, lanes],
                    out_ref.at[step, 0, :, pl.ds(pl.multiple_of(start + j * tile, LANES), tile)],
                    done.at[step, j],
                )
            )
            copies[-1].start()
    for copy in copies:
        copy.wait()


def place_kernel(quarter, core_ref, piece_ref, buffer_ref, out_ref, done):
    steps, _, width = piece_ref.shape
    tile = width // TILES
    start = pl.multiple_of((1 - core_ref[0]) * (2 * width) + quarter * width, LANES)
    copies = []
    for step in range(steps):
        for j in range(TILES):
            copies.append(
                pltpu.make_async_copy(
                    piece_ref.at[step, :, pl.ds(j * tile, tile)],
                    out_ref.at[step, 0, :, pl.ds(pl.multiple_of(start + j * tile, LANES), tile)],
                    done.at[step, j],
                )
            )
            copies[-1].start()
    for copy in copies:
        copy.wait()


def shards(anchor, momentum, adam_first, adam_second, gradients, probe_tokens, matching):
    replicas = lax.axis_size("rep")
    group = lax.axis_size("fsdp")
    _, rows, columns = anchor.shape
    steps, _, tokens, depth = probe_tokens.shape
    slab = columns // SLABS
    window = LANES * (-(-slab // (2 * LANES)))
    quarter = columns // 4
    unit = rows * columns
    ring = group // 4
    place = lax.axis_index("fsdp")
    core = lax.rem(place, 2).astype(jnp.int32)
    core_ref = core[None]

    whole = pl.BlockSpec(memory_space=pltpu.VMEM)
    scalar = pl.BlockSpec(memory_space=pltpu.SMEM)
    far = pl.BlockSpec(memory_space=pltpu.HBM)
    loose = pl.BlockSpec(memory_space=pl.ANY)
    flat = jax.ShapeDtypeStruct((rows, columns), F32)
    whole_out = jax.ShapeDtypeStruct((1, rows, columns), F32)
    part = jax.ShapeDtypeStruct((steps, rows, quarter), BF16)
    chip = jax.ShapeDtypeStruct((steps, 3, rows, quarter), BF16)
    own_rows = jax.ShapeDtypeStruct((2, steps, rows, quarter), BF16)
    moved = jax.ShapeDtypeStruct((replicas, 3, rows, window), BF16)
    two_backs = jax.ShapeDtypeStruct((replicas, 2, rows, window), BF16)
    one_back = jax.ShapeDtypeStruct((replicas, rows, window), BF16)
    products = jax.ShapeDtypeStruct((steps, 1, tokens, columns), BF16)
    sent_products = jax.ShapeDtypeStruct((steps, tokens, quarter), BF16)

    def call(kernel, name, in_specs, out_specs, out_shape, flops, nbytes, limit=VMEM_LIMIT, **rest):
        return pl.pallas_call(
            kernel,
            in_specs=in_specs,
            out_specs=out_specs,
            out_shape=out_shape,
            compiler_params=params(limit),
            cost_estimate=cost(flops, nbytes),
            name=name,
            **rest,
        )

    def at(z, y, c):
        return (z * ring + y % ring) * 2 + c

    def permute(value, dz=0, dy=0, dc=0):
        pairs = [
            (at(z, y, c), at(z ^ dz, y + dy, c ^ dc))
            for z in range(2)
            for y in range(ring)
            for c in range(2)
        ]
        return lax.ppermute(value, "fsdp", pairs)

    def relayed(value):
        return lax.all_to_all(value, "rep", 0, 0, tiled=True)

    z_at, y_at = place // (2 * ring), (place // 2) % ring
    owners = jnp.stack(
        [
            ((z_at ^ dz) * ring + (y_at + dy) % ring) * 2 + (core ^ dc)
            for dy in (0, -1, 1, 2)
            for dz in range(2)
            for dc in range(2)
        ]
    )
    own_tokens = probe_tokens[:, 0]
    chip_tokens = jnp.concatenate([own_tokens, permute(own_tokens, dc=1)], axis=1)
    chip_tokens = jnp.take(
        chip_tokens.reshape(steps, 2 * tokens, group, depth // group), owners, axis=2
    ).reshape(steps, 2 * tokens, depth)

    packed, d1 = call(
        pack_kernel,
        "pack",
        [far] * 5,
        [whole] * 2,
        [moved, flat],
        100 * unit,
        26 * unit,
        PACK_LIMIT,
        scratch_shapes=[pltpu.VMEM((SLABS, rows, slab), t) for t in (F32, F32, F32, F32, BF16)]
        + [pltpu.SemaphoreType.DMA((SLABS, 5))],
    )(anchor, momentum, adam_first, adam_second, gradients)
    got = relayed(packed)
    d2 = call(second_kernel, "second", [whole] * 3, whole, flat, 120 * unit, 14 * unit)(
        adam_first, adam_second, gradients
    )

    back = call(
        relay_kernel,
        "relay",
        [scalar, whole, loose, loose],
        whole,
        two_backs,
        30 * unit,
        10 * unit,
        scratch_shapes=[pltpu.VMEM((replicas, rows, window), F32)],
    )(matching, got, d2, chip_tokens)
    kept_low, sent_low, kept_high, sent_high, own, anchor_out = call(
        weights_kernel,
        "weights",
        [scalar, whole, whole, whole],
        [whole] * 6,
        [part] * 4 + [own_rows, whole_out],
        8 * unit,
        24 * unit,
    )(core_ref, relayed(back), d1, d2)

    def to_chip(kept, sent):
        return permute(sent, dc=1), permute(kept, dz=1), permute(sent, dz=1, dc=1)

    own_up, own_down = permute(own, dy=1), permute(own, dy=-1)
    low, kept_high, sent_high = call(
        low_chip_kernel,
        "low_chip",
        [whole] * 5 + [loose] * 2,
        [whole] * 3,
        [chip, part, part],
        0,
        10 * unit,
    )(*to_chip(kept_low, sent_low), kept_high, sent_high, own_up, own_down)
    low_up, low_down = permute(low, dy=1), permute(low, dy=-1)
    high = call(chip_kernel, "chip", [whole] * 3 + [loose], whole, chip, 0, 6 * unit)(
        *to_chip(kept_high, sent_high), low_down
    )
    high_down, high_up = permute(high, dy=-1), permute(high, dy=1)
    far_rows = jax.ShapeDtypeStruct((steps, 4, rows, quarter), BF16)

    def onward(at_quarter, own, others, *after):
        kernel = functools.partial(onward_kernel, at_quarter)
        in_specs = [whole] * 2 + [loose] * len(after)
        return call(kernel, "onward", in_specs, whole, far_rows, 0, 8 * unit)(own, others, *after)

    low_onward = onward(0, own_up, low_up)
    low_far = permute(low_onward, dy=1)
    high_onward = onward(1, own_down, high_down, high_up)
    high_far = permute(high_onward, dy=-1)
    last = call(
        momentum_relay_kernel,
        "momentum_relay",
        [scalar, whole, loose, loose],
        whole,
        one_back,
        30 * unit,
        8 * unit,
        scratch_shapes=[pltpu.VMEM((replicas, rows, window), F32)],
    )(matching, got, low_onward, high)
    momentum_out = call(momentum_kernel, "momentum", [whole] * 2, whole, whole_out, 2 * unit, 10 * unit)(
        relayed(last), d2
    )

    def evaluate(at_quarter, blocks, buffer, *after):
        kernel = functools.partial(evaluate_kernel, at_quarter)
        operands = [core_ref, chip_tokens, *blocks, *after]
        in_specs = [scalar] + [whole] * 8 + [loose] * len(after)
        aliases = {}
        if buffer is not None:
            aliases = {len(operands): 0}
            operands.append(buffer)
            in_specs.append(far)
        return call(
            kernel,
            "evaluate",
            in_specs,
            [far, whole],
            [products, sent_products],
            8 * tokens * depth * quarter,
            16 * unit,
            input_output_aliases=aliases,
            scratch_shapes=[
                pltpu.VMEM((steps, tokens, quarter), BF16),
                pltpu.SemaphoreType.DMA((steps, TILES)),
            ],
        )(*operands)

    def put(at_quarter, piece, buffer):
        return call(
            functools.partial(place_kernel, at_quarter),
            "place",
            [scalar, whole, far],
            far,
            products,
            0,
            8 * unit,
            input_output_aliases={2: 0},
            scratch_shapes=[pltpu.SemaphoreType.DMA((steps, TILES))],
        )(core_ref, piece, buffer)

    lows = own, low, own_up, low_up, own_down, low_down, low_far
    highs = own, high, own_up, high_up, own_down, high_down, high_far
    buffer, low_sent = evaluate(0, lows, None, high_onward)
    buffer, high_sent = evaluate(1, highs, buffer, momentum_out)
    buffer = put(0, permute(low_sent, dc=1), buffer)
    buffer = put(1, permute(high_sent, dc=1), buffer)
    return anchor_out, momentum_out, buffer


def solution(mesh):
    placed = (
        P("rep", "fsdp", None),
        P("rep", "fsdp", None),
        P("rep", "fsdp", None),
        P("rep", "fsdp", None),
        P(None, "rep", "fsdp", None),
        P(None, "rep", "fsdp", None),
        P(),
    )
    return jax.shard_map(
        shards,
        mesh=mesh,
        in_specs=placed,
        out_specs=(P("rep", "fsdp", None), P("rep", "fsdp", None), P(None, "rep", "fsdp", None)),
        check_vma=False,
    )
```

```python
import functools

import jax
import jax.numpy as jnp
from jax import lax
from jax.experimental import pallas as pl
from jax.experimental.pallas import tpu as pltpu
from jax.sharding import PartitionSpec as P

INNER = 4
first_decay = 0.9
second_decay = 0.95
inner_rate = 0.2
weight_decay = 0.1
outer_rate = 0.7
outer_beta = 0.9
epsilon = 1e-08

SHRINK = 1.0 - inner_rate * weight_decay
KEEP = SHRINK**INNER
Z_OF_W = 1.0 - outer_rate * (1.0 - KEEP)
Z_OF_U = -outer_rate * outer_beta
Y_OF_W = 1.0 - KEEP
Y_OF_U = outer_beta

LANES = 128
SLABS = 8
F32 = jnp.float32
BF16 = jnp.bfloat16
VMEM_LIMIT = 14 * 1024 * 1024
PACK_LIMIT = 58 * 1024 * 1024


def params(limit=VMEM_LIMIT):
    return pltpu.CompilerParams(vmem_limit_bytes=limit)


def cost(flops, moved):
    return pl.CostEstimate(flops=int(flops), bytes_accessed=int(moved), transcendentals=0)


def adam(first, second, gradient):
    moved = (1.0 - first_decay) * gradient
    squared = (1.0 - second_decay) * gradient * gradient
    total = None
    for inner_pass in range(INNER):
        first = first_decay * first + moved
        second = second_decay * second + squared
        step = first / (jnp.sqrt(second) + epsilon)
        total = step if total is None else SHRINK * total + step
    return first, second, inner_rate * total


def windows(columns, window):
    slab = columns // SLABS
    return [start for j in range(SLABS) for start in (j * slab, (j + 1) * slab - window)]


def pack_kernel(*refs):
    sources, (packed_ref, d_out), held, arrived = refs[:5], refs[5:7], refs[7:12], refs[12]
    columns, window = d_out.shape[1], packed_ref.shape[3]
    slab = columns // SLABS
    starts = windows(columns, window)
    copies = []
    for j in range(SLABS):
        lanes = pl.ds(j * slab, slab)
        for i, (source, kept) in enumerate(zip(sources, held)):
            piece = source.at[0, 0, :, lanes] if i == 4 else source.at[0, :, lanes]
            copies.append(pltpu.make_async_copy(piece, kept.at[j], arrived.at[j, i]))
            copies[-1].start()
    for j in range(SLABS):
        lanes = pl.ds(j * slab, slab)
        for copy in copies[5 * j : 5 * j + 5]:
            copy.wait()
        w, u, m, v, g = (kept[j] for kept in held)
        d = adam(m, v, g.astype(F32))[2]
        d_out[:, lanes] = d
        sent = (Z_OF_W * w + Z_OF_U * u, Y_OF_U * u + Y_OF_W * w, d)
        for relay in (2 * j, 2 * j + 1):
            start = starts[relay] - j * slab
            for which, value in enumerate(sent):
                packed_ref[relay, which] = value[:, start : start + window].astype(BF16)


def second_kernel(m_ref, v_ref, g_ref, d_out):
    columns = d_out.shape[1]
    slab = columns // SLABS
    for j in range(SLABS):
        lanes = pl.ds(j * slab, slab)
        first, second = m_ref[0, :, lanes], v_ref[0, :, lanes]
        gradient = g_ref[0, 0, :, lanes].astype(F32)
        for _ in range(INNER):
            first = first_decay * first + (1.0 - first_decay) * gradient
            second = second_decay * second + (1.0 - second_decay) * gradient * gradient
        d_out[:, lanes] = adam(first, second, g_ref[1, 0, :, lanes].astype(F32))[2]


def mean(got_ref, which, r, p):
    return 0.5 * (got_ref[r, which].astype(F32) + got_ref[p, which].astype(F32))


def after_first_step(got_ref, r, p, of_w, of_u):
    shared = mean(got_ref, 0, r, p)
    d = got_ref[r, 2].astype(F32)
    return of_w * (shared - outer_rate * d) + of_u * (mean(got_ref, 1, r, p) + d), shared


def relay_kernel(matching_ref, got_ref, d_ref, tokens_ref, back_ref, held_ref):
    replicas = got_ref.shape[0]

    @pl.loop(0, replicas)
    def _(r):
        held_ref[r], shared = after_first_step(got_ref, r, matching_ref[0, r], Z_OF_W, Z_OF_U)
        back_ref[r, 0] = shared.astype(BF16)

    @pl.loop(0, replicas)
    def _(r):
        back_ref[r, 1] = (0.5 * (held_ref[r] + held_ref[matching_ref[1, r]])).astype(BF16)


def momentum_relay_kernel(matching_ref, got_ref, *refs):
    back_ref, held_ref = refs[-2:]
    replicas = got_ref.shape[0]

    @pl.loop(0, replicas)
    def _(r):
        held_ref[r] = after_first_step(got_ref, r, matching_ref[0, r], Y_OF_W, Y_OF_U)[0]

    @pl.loop(0, replicas)
    def _(r):
        back_ref[r] = (0.5 * (held_ref[r] + held_ref[matching_ref[1, r]])).astype(BF16)


def joined(first, last, slab):
    overlap = first.shape[1] + last.shape[1] - slab
    return jnp.concatenate([first, last[:, overlap:]], axis=1).astype(F32)


def weights_kernel(core_ref, back_ref, d1_ref, d2_ref, *refs):
    parts, (own_ref, w_ref) = refs[:4], refs[4:]
    slab = d1_ref.shape[1] // SLABS
    for j in range(SLABS):
        lanes = pl.ds(j * slab, slab)
        first, second = (joined(back_ref[2 * j, i], back_ref[2 * j + 1, i], slab) for i in range(2))
        first = first - outer_rate * d1_ref[:, lanes]
        second = second - outer_rate * d2_ref[:, lanes]
        w_ref[0, :, lanes] = second
        quarter, lanes = j % (SLABS // 2) // 2, pl.ds(j % 2 * slab, slab)
        mine = core_ref[0] == j // (SLABS // 2)
        for away, chosen in enumerate((mine, jnp.logical_not(mine))):
            part = parts[2 * quarter + away]

            @pl.when(chosen)
            def _(part=part, lanes=lanes, first=first, second=second):
                part[0, :, lanes] = first.astype(BF16)
                part[1, :, lanes] = second.astype(BF16)

        @pl.when(mine)
        def _(quarter=quarter, lanes=lanes, first=first, second=second):
            own_ref[quarter, 0, :, lanes] = first.astype(BF16)
            own_ref[quarter, 1, :, lanes] = second.astype(BF16)


def momentum_kernel(back_ref, d_ref, u_ref):
    slab = d_ref.shape[1] // SLABS
    for j in range(SLABS):
        lanes = pl.ds(j * slab, slab)
        u_ref[0, :, lanes] = joined(back_ref[2 * j], back_ref[2 * j + 1], slab) + d_ref[:, lanes]


def onward_kernel(quarter, own_ref, others_ref, *refs):
    out_ref = refs[-1]
    for step in range(out_ref.shape[0]):
        out_ref[step, 0] = own_ref[quarter, step]
        for i in range(3):
            out_ref[step, i + 1] = others_ref[step, i]


def low_chip_kernel(*refs):
    chip_kernel(*refs[:3], refs[-3])
    for part, later in zip(refs[3:5], refs[-2:]):
        later[...] = part[...]


def chip_kernel(*refs):
    pieces, out = refs[:3], refs[-1]
    for i, piece in enumerate(pieces):
        for step in range(out.shape[0]):
            out[step, i] = piece[step]


TILES = 5


def evaluate_kernel(quarter, core_ref, tokens_ref, *refs):
    blocks, far_ref, (out_ref, sent_ref, own_ref, done) = refs[:6], refs[6], refs[-4:]
    steps, tokens, width = sent_ref.shape
    tile = width // TILES
    start = pl.multiple_of(core_ref[0] * (2 * width) + quarter * width, LANES)
    copies = []
    for step in range(steps):
        for j in range(TILES):
            lanes = pl.ds(j * tile, tile)
            rows = []
            for own, others in zip(blocks[::2], blocks[1::2]):
                rows.append(own[quarter, step, :, lanes])
                rows += [others[step, i, :, lanes] for i in range(3)]
            rows += [far_ref[step, i, :, lanes] for i in range(4)]
            rows = jnp.concatenate(rows, axis=0)
            product = jnp.dot(tokens_ref[step], rows, preferred_element_type=F32).astype(BF16)
            own_ref[step, :, lanes] = product[:tokens]
            sent_ref[step, :, lanes] = product[tokens:]
            copies.append(
                pltpu.make_async_copy(
                    own_ref.at[step, :, lanes],
                    out_ref.at[step, 0, :, pl.ds(pl.multiple_of(start + j * tile, LANES), tile)],
                    done.at[step, j],
                )
            )
            copies[-1].start()
    for copy in copies:
        copy.wait()


def place_kernel(quarter, core_ref, piece_ref, buffer_ref, out_ref, done):
    steps, _, width = piece_ref.shape
    tile = width // TILES
    start = pl.multiple_of((1 - core_ref[0]) * (2 * width) + quarter * width, LANES)
    copies = []
    for step in range(steps):
        for j in range(TILES):
            copies.append(
                pltpu.make_async_copy(
                    piece_ref.at[step, :, pl.ds(j * tile, tile)],
                    out_ref.at[step, 0, :, pl.ds(pl.multiple_of(start + j * tile, LANES), tile)],
                    done.at[step, j],
                )
            )
            copies[-1].start()
    for copy in copies:
        copy.wait()


def shards(anchor, momentum, adam_first, adam_second, gradients, probe_tokens, matching):
    replicas = lax.axis_size("rep")
    group = lax.axis_size("fsdp")
    _, rows, columns = anchor.shape
    steps, _, tokens, depth = probe_tokens.shape
    slab = columns // SLABS
    window = LANES * (-(-slab // (2 * LANES)))
    quarter = columns // 4
    unit = rows * columns
    ring = group // 4
    place = lax.axis_index("fsdp")
    core = lax.rem(place, 2).astype(jnp.int32)
    core_ref = core[None]

    whole = pl.BlockSpec(memory_space=pltpu.VMEM)
    scalar = pl.BlockSpec(memory_space=pltpu.SMEM)
    far = pl.BlockSpec(memory_space=pltpu.HBM)
    loose = pl.BlockSpec(memory_space=pl.ANY)
    flat = jax.ShapeDtypeStruct((rows, columns), F32)
    whole_out = jax.ShapeDtypeStruct((1, rows, columns), F32)
    part = jax.ShapeDtypeStruct((steps, rows, quarter), BF16)
    chip = jax.ShapeDtypeStruct((steps, 3, rows, quarter), BF16)
    own_rows = jax.ShapeDtypeStruct((2, steps, rows, quarter), BF16)
    moved = jax.ShapeDtypeStruct((replicas, 3, rows, window), BF16)
    two_backs = jax.ShapeDtypeStruct((replicas, 2, rows, window), BF16)
    one_back = jax.ShapeDtypeStruct((replicas, rows, window), BF16)
    products = jax.ShapeDtypeStruct((steps, 1, tokens, columns), BF16)
    sent_products = jax.ShapeDtypeStruct((steps, tokens, quarter), BF16)

    def call(kernel, name, in_specs, out_specs, out_shape, flops, nbytes, limit=VMEM_LIMIT, **rest):
        return pl.pallas_call(
            kernel,
            in_specs=in_specs,
            out_specs=out_specs,
            out_shape=out_shape,
            compiler_params=params(limit),
            cost_estimate=cost(flops, nbytes),
            name=name,
            **rest,
        )

    def at(z, y, c):
        return (z * ring + y % ring) * 2 + c

    def permute(value, dz=0, dy=0, dc=0):
        pairs = [
            (at(z, y, c), at(z ^ dz, y + dy, c ^ dc))
            for z in range(2)
            for y in range(ring)
            for c in range(2)
        ]
        return lax.ppermute(value, "fsdp", pairs)

    def relayed(value):
        return lax.all_to_all(value, "rep", 0, 0, tiled=True)

    z_at, y_at = place // (2 * ring), (place // 2) % ring
    owners = jnp.stack(
        [
            ((z_at ^ dz) * ring + (y_at + dy) % ring) * 2 + (core ^ dc)
            for dy in (0, -1, 1, 2)
            for dz in range(2)
            for dc in range(2)
        ]
    )
    own_tokens = probe_tokens[:, 0]
    chip_tokens = jnp.concatenate([own_tokens, permute(own_tokens, dc=1)], axis=1)
    chip_tokens = jnp.take(
        chip_tokens.reshape(steps, 2 * tokens, group, depth // group), owners, axis=2
    ).reshape(steps, 2 * tokens, depth)

    packed, d1 = call(
        pack_kernel,
        "pack",
        [far] * 5,
        [whole] * 2,
        [moved, flat],
        100 * unit,
        26 * unit,
        PACK_LIMIT,
        scratch_shapes=[pltpu.VMEM((SLABS, rows, slab), t) for t in (F32, F32, F32, F32, BF16)]
        + [pltpu.SemaphoreType.DMA((SLABS, 5))],
    )(anchor, momentum, adam_first, adam_second, gradients)
    got = relayed(packed)
    d2 = call(second_kernel, "second", [whole] * 3, whole, flat, 120 * unit, 14 * unit)(
        adam_first, adam_second, gradients
    )

    back = call(
        relay_kernel,
        "relay",
        [scalar, whole, loose, loose],
        whole,
        two_backs,
        30 * unit,
        10 * unit,
        scratch_shapes=[pltpu.VMEM((replicas, rows, window), F32)],
    )(matching, got, d2, chip_tokens)
    kept_low, sent_low, kept_high, sent_high, own, anchor_out = call(
        weights_kernel,
        "weights",
        [scalar, whole, whole, whole],
        [whole] * 6,
        [part] * 4 + [own_rows, whole_out],
        8 * unit,
        24 * unit,
    )(core_ref, relayed(back), d1, d2)

    def to_chip(kept, sent):
        return permute(sent, dc=1), permute(kept, dz=1), permute(sent, dz=1, dc=1)

    own_up, own_down = permute(own, dy=1), permute(own, dy=-1)
    low, kept_high, sent_high = call(
        low_chip_kernel,
        "low_chip",
        [whole] * 5 + [loose] * 2,
        [whole] * 3,
        [chip, part, part],
        0,
        10 * unit,
    )(*to_chip(kept_low, sent_low), kept_high, sent_high, own_up, own_down)
    low_up, low_down = permute(low, dy=1), permute(low, dy=-1)
    high = call(chip_kernel, "chip", [whole] * 3, whole, chip, 0, 6 * unit)(*to_chip(kept_high, sent_high))
    high_down, high_up = permute(high, dy=-1), permute(high, dy=1)
    far_rows = jax.ShapeDtypeStruct((steps, 4, rows, quarter), BF16)

    def onward(at_quarter, own, others, *after):
        kernel = functools.partial(onward_kernel, at_quarter)
        in_specs = [whole] * 2 + [loose] * len(after)
        return call(kernel, "onward", in_specs, whole, far_rows, 0, 8 * unit)(own, others, *after)

    low_onward = onward(0, own_up, low_up, low_down)
    low_far = permute(low_onward, dy=1)
    high_onward = onward(1, own_down, high_down, high_up)
    high_far = permute(high_onward, dy=-1)
    last = call(
        momentum_relay_kernel,
        "momentum_relay",
        [scalar, whole, loose, loose],
        whole,
        one_back,
        30 * unit,
        8 * unit,
        scratch_shapes=[pltpu.VMEM((replicas, rows, window), F32)],
    )(matching, got, low_onward, high)
    momentum_out = call(momentum_kernel, "momentum", [whole] * 2, whole, whole_out, 2 * unit, 10 * unit)(
        relayed(last), d2
    )

    def evaluate(at_quarter, blocks, buffer, *after):
        kernel = functools.partial(evaluate_kernel, at_quarter)
        operands = [core_ref, chip_tokens, *blocks, *after]
        in_specs = [scalar] + [whole] * 8 + [loose] * len(after)
        aliases = {}
        if buffer is not None:
            aliases = {len(operands): 0}
            operands.append(buffer)
            in_specs.append(far)
        return call(
            kernel,
            "evaluate",
            in_specs,
            [far, whole],
            [products, sent_products],
            8 * tokens * depth * quarter,
            16 * unit,
            input_output_aliases=aliases,
            scratch_shapes=[
                pltpu.VMEM((steps, tokens, quarter), BF16),
                pltpu.SemaphoreType.DMA((steps, TILES)),
            ],
        )(*operands)

    def put(at_quarter, piece, buffer):
        return call(
            functools.partial(place_kernel, at_quarter),
            "place",
            [scalar, whole, far],
            far,
            products,
            0,
            8 * unit,
            input_output_aliases={2: 0},
            scratch_shapes=[pltpu.SemaphoreType.DMA((steps, TILES))],
        )(core_ref, piece, buffer)

    lows = own, low, own_up, low_up, own_down, low_down, low_far
    highs = own, high, own_up, high_up, own_down, high_down, high_far
    buffer, low_sent = evaluate(0, lows, None, high_onward)
    buffer, high_sent = evaluate(1, highs, buffer, momentum_out)
    buffer = put(0, permute(low_sent, dc=1), buffer)
    buffer = put(1, permute(high_sent, dc=1), buffer)
    return anchor_out, momentum_out, buffer


def solution(mesh):
    placed = (
        P("rep", "fsdp", None),
        P("rep", "fsdp", None),
        P("rep", "fsdp", None),
        P("rep", "fsdp", None),
        P(None, "rep", "fsdp", None),
        P(None, "rep", "fsdp", None),
        P(),
    )
    return jax.shard_map(
        shards,
        mesh=mesh,
        in_specs=placed,
        out_specs=(P("rep", "fsdp", None), P("rep", "fsdp", None), P(None, "rep", "fsdp", None)),
        check_vma=False,
    )
```
